32 devices in a mesh: groups: 1, ctx: 32 (over z, y, x, core).
Axes of the slice: x: 2, y: 2, z: 4, core: 2. Of those that a mesh axis runs over, the one named last changes fastest.
Arguments:
- hidden_in: bfloat16 [4096, 4096], P(('groups', 'ctx')), may hold values from -64 to 64
- in_weight: bfloat16 [32, 128, 384], replicated, may hold values from -0.5 to 0.5
- feat_filter: float32 [3, 12288], replicated, may hold values from -3 to 3
- inner_filter: float32 [7, 4096], replicated, may hold values from -3 to 3
- norm_gain: float32 [4096], replicated, may hold values from 0.5 to 1.5
- attn_weight: bfloat16 [3, 32, 128, 128], replicated, may hold values from -3 to 3, as said below
- doc_lengths: int32 [8], P('groups'), may hold values from 1 to 8, as said below
Outputs:
- output: bfloat16 [4096, 4096], P(('groups', 'ctx'))
The draws below stay inside these ranges and needn't reach their ends.
Inputs may be any that keep to these rules, and one draw needn't show every extreme that they name: Documents start at 128 times the running sums of doc_lengths and fill the sequence; the longest document is exactly 1024 tokens. `attn_weight`: Query, key and value maps in that order along the first dimension.
All inputs are finite; a program needn't handle non-finite values.
Results may differ from the reference program's by a relative error of at most 0.006.
The reference program's roundings to bfloat16 on the way (of `streams`, `gated_rows`, `residual`, `normed`, `projected` and `weights_bf`) count: a program that leaves them out, or rounds other values in their place, can miss the bound.
Values may be sent and summed in bfloat16 or wider, within the bound.
A program may use at most 128 MiB of HBM per device.

```python
import jax
import jax.numpy as jnp
from jax import lax

HEADS = 32
HD = 128
FEAT = 3
FILT = 7
BLOCK = 128
TOK_DEV = 128
CHANNELS = 4096
TOKENS = 4096
NBLK = 32
MBLK = 8
NDOCS = 8
REACH = 7


def draw_hidden_in(key, part):
    key_a, key_b, key_c = jax.random.split(key, 3)
    row_scale = jnp.exp(jax.random.uniform(key_b, (TOKENS, 1), jnp.float32, jnp.log(0.3), jnp.log(3.0)))
    col_scale = jnp.exp(jax.random.uniform(key_c, (1, CHANNELS), jnp.float32, jnp.log(0.3), jnp.log(3.0)))
    base_vals = jax.random.normal(key_a, (TOKENS, CHANNELS), jnp.float32)
    return (base_vals * row_scale * col_scale).astype(jnp.bfloat16)


def draw_attn_weight(key, part):
    key_a, key_b, key_c = jax.random.split(key, 3)
    scaling = HD ** (-0.5)
    query_map = jax.random.normal(key_a, (HEADS, HD, HD), jnp.float32) * scaling
    key_map = jax.random.normal(key_b, (HEADS, HD, HD), jnp.float32) * scaling
    value_map = jax.random.normal(key_c, (HEADS, HD, HD), jnp.float32) * scaling
    return jnp.stack([query_map, key_map, value_map], axis=0).astype(jnp.bfloat16)


def draw_doc_lengths(key, part):
    key_a, key_b = jax.random.split(jax.random.fold_in(key, 7), 2)
    segments = NBLK // MBLK
    first_part = jax.random.randint(key_a, (segments,), 1, MBLK, dtype=jnp.int32)
    second_part = MBLK - first_part
    lengths = jnp.stack([first_part, second_part], axis=1).reshape(NDOCS)
    lengths = lengths.at[NDOCS - 2].set(1)
    lengths = lengths.at[NDOCS - 1].set(MBLK - 1)
    middle_seg = NBLK // 2 // MBLK
    inner_len = jax.random.randint(key_b, (), 1, MBLK - 1, dtype=jnp.int32)
    lengths = lengths.at[2 * (middle_seg - 1)].set(1)
    lengths = lengths.at[2 * (middle_seg - 1) + 1].set(MBLK)
    lengths = lengths.at[2 * middle_seg].set(inner_len)
    lengths = lengths.at[2 * middle_seg + 1].set(MBLK - 1 - inner_len)
    return lengths.astype(jnp.int32)


def gaussian(rng, extent, deviation, limit, kind=jnp.bfloat16):
    array = jax.random.normal(rng, extent, jnp.float32) * deviation
    return jnp.minimum(jnp.maximum(array, -limit), limit).astype(kind)


def setup_inputs(seed: int = 0, part: int = 0) -> dict:
    streams_of = jax.random.split(jax.random.key(seed), 8)
    part_keys = jax.random.split(jax.random.fold_in(streams_of[7], part), 8)
    return {
        "hidden_in": draw_hidden_in(jax.random.fold_in(jax.random.fold_in(streams_of[7], part), 71), part),
        "in_weight": gaussian(streams_of[1], (HEADS, HD, 3 * HD), HD ** -0.5, 0.5),
        "feat_filter": gaussian(streams_of[2], (FEAT, 3 * CHANNELS), 0.5, 3.0, jnp.float32),
        "inner_filter": gaussian(streams_of[3], (FILT, CHANNELS), 0.4, 3.0, jnp.float32),
        "norm_gain": jnp.clip(1.0 + 0.1 * jax.random.normal(streams_of[4], (CHANNELS,), jnp.float32), 0.5, 1.5),
        "attn_weight": draw_attn_weight(jax.random.fold_in(streams_of[7], 71), part),
        "doc_lengths": draw_doc_lengths(jax.random.fold_in(jax.random.fold_in(streams_of[7], part), 71), part),
    }


def rounded(value):
    return lax.optimization_barrier(value.astype(jnp.bfloat16))

def doc_start(positions, doc_lengths):
    doc_ends = jnp.cumsum(doc_lengths).astype(jnp.int32) * BLOCK
    passed = doc_ends[None, :] <= positions[:, None]
    return lax.optimization_barrier(jnp.sum(jnp.where(passed, doc_lengths[None, :] * BLOCK, 0), axis=1)).astype(jnp.int32)

def causal_taps(series, filter_taps, out_positions, out_begin):
    tap_count = filter_taps.shape[0]
    out_count = out_positions.shape[0]
    summed = jnp.zeros((out_count, series.shape[1]), jnp.float32)
    for shift_by in range(tap_count):
        shifted = series[tap_count - 1 - shift_by:tap_count - 1 - shift_by + out_count].astype(jnp.float32)
        allowed = (out_positions - shift_by >= out_begin)[:, None]
        summed = summed + jnp.where(allowed, shifted * filter_taps[shift_by][None, :], 0.0)
    return summed

def attend(query_group, key_group, value_group, visible):
    scores = jnp.einsum('thd,lhd->htl', query_group, key_group) * HD ** (-0.5)
    scores = jnp.where(visible[None], scores, -1e+30)
    row_top = lax.optimization_barrier(jnp.max(scores, axis=-1, keepdims=True))
    exps = jnp.exp(scores - row_top)
    summed = lax.optimization_barrier(jnp.sum(exps, axis=-1))
    weights_bf = rounded(exps)
    attended = jnp.einsum('htl,lhd->thd', weights_bf.astype(jnp.float32), value_group)
    return attended / jnp.transpose(summed)[:, :, None]

def reference(hidden_in, in_weight, feat_filter, inner_filter, norm_gain, attn_weight, doc_lengths):
    tok_total = hidden_in.shape[0]
    channels = hidden_in.shape[1]
    positions = jnp.arange(tok_total, dtype=jnp.int32)
    doc_begin = doc_start(positions, doc_lengths)
    head_inputs = jnp.transpose(hidden_in.reshape(tok_total, HEADS, HD), (1, 0, 2))
    head_feats = jnp.transpose(feat_filter.reshape(FEAT, HEADS, 3 * HD), (1, 0, 2))
    head_inners = jnp.transpose(inner_filter.reshape(FILT, HEADS, HD), (1, 0, 2))

    def per_head(operands):
        head_input, head_weight, head_feat, head_inner = operands
        streams = rounded(jnp.dot(head_input, head_weight, preferred_element_type=jnp.float32))
        padded = jnp.concatenate([jnp.zeros((FEAT - 1, 3 * HD), jnp.bfloat16), streams], axis=0)
        features = causal_taps(padded, head_feat, positions, doc_begin)
        gated_rows = rounded(features[:, HD:2 * HD] * features[:, 2 * HD:])
        padded = jnp.concatenate([jnp.zeros((FILT - 1, HD), jnp.bfloat16), gated_rows], axis=0)
        convolved = causal_taps(padded, head_inner, positions, doc_begin)
        return features[:, :HD] * convolved
    mixing = lax.map(per_head, (head_inputs, in_weight, head_feats, head_inners))
    mixing = jnp.transpose(mixing, (1, 0, 2)).reshape(tok_total, channels)
    residual = rounded(hidden_in.astype(jnp.float32) + mixing)
    res_float = residual.astype(jnp.float32)
    normed = rounded(res_float * lax.rsqrt(lax.optimization_barrier(jnp.mean(res_float * res_float, axis=-1, keepdims=True)) + 1e-05) * norm_gain[None, :])
    projected = rounded(jnp.einsum('thd,shde->sthe', normed.reshape(tok_total, HEADS, HD).astype(jnp.float32), attn_weight.astype(jnp.float32)))
    key_span = (REACH + 1) * TOK_DEV
    key_rows = jnp.concatenate([jnp.zeros((REACH * TOK_DEV, HEADS, HD), jnp.bfloat16), projected[1]], axis=0)
    value_rows = jnp.concatenate([jnp.zeros((REACH * TOK_DEV, HEADS, HD), jnp.bfloat16), projected[2]], axis=0)
    blocks = tok_total // TOK_DEV

    def one_block(block_index):
        block_first = (block_index * TOK_DEV).astype(jnp.int32)
        queries = lax.dynamic_slice_in_dim(projected[0], block_first, TOK_DEV, 0).astype(jnp.float32)
        key_group = lax.dynamic_slice_in_dim(key_rows, block_first, key_span, 0).astype(jnp.float32)
        value_group = lax.dynamic_slice_in_dim(value_rows, block_first, key_span, 0).astype(jnp.float32)
        query_pos = block_first + jnp.arange(TOK_DEV, dtype=jnp.int32)
        key_pos = block_first - REACH * TOK_DEV + jnp.arange(key_span, dtype=jnp.int32)
        query_begin = lax.dynamic_slice_in_dim(doc_begin, block_first, TOK_DEV, 0)
        visible = (key_pos[None, :] >= query_begin[:, None]) & (key_pos[None, :] <= query_pos[:, None])
        return attend(queries, key_group, value_group, visible)
    attended = lax.map(one_block, jnp.arange(blocks, dtype=jnp.int32))
    attended = attended.reshape(tok_total, channels)
    return (res_float + attended).astype(jnp.bfloat16)
```

```python
import functools

import jax
import jax.numpy as jnp
from jax import lax
from jax.experimental import pallas as pl
from jax.experimental.pallas import tpu as pltpu
from jax.sharding import PartitionSpec as P

GROUP = 8
HALO = 16
MESH = pl.DeviceIdType.MESH
F32 = jnp.float32
BF16 = jnp.bfloat16
NEG = -1e30


def remote(src, dst, send_sem, recv_sem, device):
    return pltpu.make_async_remote_copy(
        src_ref=src,
        dst_ref=dst,
        send_sem=send_sem,
        recv_sem=recv_sem,
        device_id={"ctx": device},
        device_id_type=MESH,
    )


def kernel(
    ctx,
    doc_ref,
    hid,
    in_w,
    feat_ref,
    inner_ref,
    gain_ref,
    attn_w,
    out,
    x_ext,
    w_in,
    w_attn,
    res_send,
    res_own,
    res_prev,
    sc_send,
    sc_own,
    sc_prev,
    ssq,
    q_own,
    k_own,
    v_own,
    k_prev,
    v_prev,
    acc_ref,
    m_ref,
    l_ref,
    out_buf,
    load_sem,
    halo_sem,
    next_send,
    own_send,
    own_recv,
    prev_recv,
    next_sc_send,
    own_sc_send,
    own_sc_recv,
    prev_sc_recv,
    out_send,
    out_recv,
    own_sem,
):
    tok, channels = hid.shape
    hd = w_in.shape[1]
    heads = w_in.shape[0]
    per = heads // GROUP
    wide = per * hd
    taps = feat_ref.shape[0]
    inner_taps = inner_ref.shape[0]
    me = lax.axis_index("ctx")
    r = lax.rem(me, GROUP)
    group = lax.div(me, GROUP)
    base = group * GROUP
    has_prev = group > 0
    has_next = group < ctx // GROUP - 1

    loads = [
        pltpu.make_async_copy(hid, x_ext.at[pl.ds(HALO, tok)], load_sem.at[0]),
        pltpu.make_async_copy(in_w, w_in, load_sem.at[1]),
    ]
    for s in range(3):
        loads.append(
            pltpu.make_async_copy(
                attn_w.at[s, pl.ds(r * per, per)],
                w_attn.at[:, :, pl.ds(s * hd, hd)],
                load_sem.at[2 + s],
            )
        )
    for copy in loads:
        copy.start()

    barrier = pltpu.get_barrier_semaphore()

    def signal_own(j, carry):
        @pl.when(j != r)
        def _():
            pl.semaphore_signal(
                barrier, inc=1, device_id={"ctx": base + j}, device_id_type=MESH
            )

        @pl.when(has_prev)
        def _():
            pl.semaphore_signal(
                barrier, inc=1, device_id={"ctx": base - GROUP + j}, device_id_type=MESH
            )

        return carry

    lax.fori_loop(0, GROUP, signal_own, 0)

    @pl.when(has_next)
    def _():
        pl.semaphore_wait(barrier, 2 * GROUP - 1)

    @pl.when(jnp.logical_not(has_next))
    def _():
        pl.semaphore_wait(barrier, GROUP - 1)

    halo = remote(
        hid.at[pl.ds(tok - HALO, HALO)],
        x_ext.at[pl.ds(0, HALO)],
        halo_sem.at[0],
        halo_sem.at[1],
        lax.rem(me + 1, ctx),
    )

    @pl.when(me < ctx - 1)
    def _():
        halo.start()

    def doc_step(d, carry):
        end = carry[0] + doc_ref[d]
        return (end,) + tuple(
            jnp.where(end <= block, end, begin)
            for begin, block in zip(carry[1:], [base + t for t in range(GROUP)] + [me])
        )

    zero = jnp.int32(0)
    found = lax.fori_loop(0, doc_ref.shape[0], doc_step, (zero,) * (GROUP + 2))
    begins = found[1 : GROUP + 1]
    my_begin = found[GROUP + 1]

    loads[0].wait()
    loads[1].wait()

    @pl.when(me > 0)
    def _():
        halo.wait_recv()

    @pl.when(me == 0)
    def _():
        x_ext[0:HALO, :] = jnp.zeros((HALO, channels), BF16)

    keep = jnp.where(my_begin < me, 1.0, 0.0).astype(F32)
    x_ext[0:HALO, :] = (x_ext[0:HALO, :].astype(F32) * keep).astype(BF16)

    ssq[...] = jnp.zeros_like(ssq)

    def mix_chunk(step, carry):
        chunk = lax.rem(r + 1 + step, GROUP)
        total = ssq[...]
        for hh in range(per):
            head = chunk * per + hh
            x = x_ext[:, pl.ds(pl.multiple_of(head * hd, hd), hd)]
            streams = jnp.dot(x, w_in[head], preferred_element_type=F32).astype(BF16).astype(F32)
            taps_f = feat_ref[:, pl.ds(pl.multiple_of(head * 3 * hd, 3 * hd), 3 * hd)]
            feats = streams * taps_f[0:1]
            for t in range(1, taps):
                feats = feats + pltpu.roll(streams, t, 0) * taps_f[t : t + 1]
            gated = (feats[:, hd : 2 * hd] * feats[:, 2 * hd :]).astype(BF16).astype(F32)
            taps_i = inner_ref[:, pl.ds(pl.multiple_of(head * hd, hd), hd)]
            conv = gated * taps_i[0:1]
            for t in range(1, inner_taps):
                conv = conv + pltpu.roll(gated, t, 0) * taps_i[t : t + 1]
            residual = (x[HALO:].astype(F32) + feats[HALO:, :hd] * conv[HALO:]).astype(BF16)
            res_send[chunk, :, hh * hd : (hh + 1) * hd] = residual
            res_float = residual.astype(F32)
            total = total + res_float * res_float
        ssq[...] = total

        @pl.when(has_next)
        def _():
            remote(
                res_send.at[chunk],
                res_prev.at[r],
                next_send.at[chunk],
                prev_recv.at[r],
                base + GROUP + chunk,
            ).start()

        @pl.when(chunk != r)
        def _():
            remote(
                res_send.at[chunk],
                res_own.at[r],
                own_send.at[chunk],
                own_recv.at[r],
                base + chunk,
            ).start()

        return carry

    lax.fori_loop(0, GROUP, mix_chunk, 0)
    keep_own = pltpu.make_async_copy(res_send.at[r], res_own.at[r], own_sem.at[0])
    keep_own.start()

    mean = jnp.sum(ssq[...], axis=-1, keepdims=True) * (1.0 / channels)
    scale = lax.rsqrt(mean + 1e-05)
    sc_send[...] = jnp.transpose(jnp.broadcast_to(scale, (tok, tok)))[0:8]

    def send_scale(j, carry):
        @pl.when(has_next)
        def _():
            remote(
                sc_send, sc_prev.at[r], next_sc_send.at[j], prev_sc_recv.at[r], base + GROUP + j
            ).start()

        @pl.when(j != r)
        def _():
            remote(sc_send, sc_own.at[r], own_sc_send.at[j], own_sc_recv.at[r], base + j).start()

        return carry

    lax.fori_loop(0, GROUP, send_scale, 0)
    sc_own[r] = sc_send[...]
    keep_own.wait()
    for copy in loads[2:]:
        copy.wait()
    gain = gain_ref[:, pl.ds(pl.multiple_of(r * wide, wide), wide)]

    def norm_head(res_tile, scales, hh):
        columns = slice(hh * hd, (hh + 1) * hd)
        return (res_tile[:, columns].astype(F32) * scales * gain[:, columns]).astype(BF16)

    def project_own(j, carry):
        @pl.when(j != r)
        def _():
            remote(res_send.at[j], res_own.at[j], own_send.at[j], own_recv.at[j], base + j).wait_recv()
            remote(sc_send, sc_own.at[j], own_sc_send.at[j], own_sc_recv.at[j], base + j).wait_recv()

        scales = jnp.transpose(jnp.broadcast_to(sc_own[j][0:1], (tok, tok)))
        tile = res_own[j]
        rows = pl.ds(pl.multiple_of(j * tok, tok), tok)
        for hh in range(per):
            normed = norm_head(tile, scales, hh)
            made = jnp.dot(normed, w_attn[hh], preferred_element_type=F32).astype(BF16)
            q_own[hh, rows, :] = made[:, :hd]
            k_own[hh, rows, :] = made[:, hd : 2 * hd]
            v_own[hh, rows, :] = made[:, 2 * hd :]
        return carry

    lax.fori_loop(0, GROUP, project_own, 0)

    slope = hd ** (-0.5)
    contract_last = (((1,), (1,)), ((), ()))

    def score(q, k):
        return lax.dot_general(q, k, contract_last, preferred_element_type=F32)

    def hidden_bias(first, count, begin_row):
        columns = first + lax.broadcasted_iota(jnp.int32, (1, count), 1)
        return jnp.where(columns >= begin_row, 0.0, NEG).astype(F32)

    def finish(hh, t, acc, total):
        columns = pl.ds(pl.multiple_of(hh * hd, hd), hd)
        res_float = res_own[t, :, columns].astype(F32)
        out_buf[t, :, columns] = (res_float + acc * (1.0 / total)).astype(BF16)

    def send_out(t):
        columns = pl.ds(pl.multiple_of(r * wide, wide), wide)

        @pl.when(r != t)
        def _():
            remote(
                out_buf.at[t], out.at[:, columns], out_send.at[t], out_recv.at[r], base + t
            ).start()

        @pl.when(r == t)
        def _():
            pltpu.make_async_copy(out_buf.at[t], out.at[:, columns], own_sem.at[1]).start()

    tri = lax.broadcasted_iota(jnp.int32, (tok, tok), 0) >= lax.broadcasted_iota(
        jnp.int32, (tok, tok), 1
    )

    for t in range(GROUP - 1, -1, -1):
        bias = hidden_bias(0, t * tok, (begins[t] - base) * tok) if t else None

        def own_head(hh, carry, t=t, bias=bias):
            q = q_own[hh, t * tok : (t + 1) * tok, :]
            diag = jnp.where(tri, score(q, k_own[hh, t * tok : (t + 1) * tok, :]), NEG)
            top = jnp.max(diag, axis=-1, keepdims=True)
            if t:
                bulk = score(q, k_own[hh, : t * tok, :]) + bias
                top = jnp.maximum(top, jnp.max(bulk, axis=-1, keepdims=True))
            exps = jnp.exp((diag - top) * slope)
            total = jnp.sum(exps, axis=-1, keepdims=True)
            acc = jnp.dot(
                exps.astype(BF16), v_own[hh, t * tok : (t + 1) * tok, :], preferred_element_type=F32
            )
            if t:
                exps = jnp.exp((bulk - top) * slope)
                total = total + jnp.sum(exps, axis=-1, keepdims=True)
                acc = acc + jnp.dot(
                    exps.astype(BF16), v_own[hh, : t * tok, :], preferred_element_type=F32
                )
            if t == GROUP - 1:
                finish(hh, t, acc, total)
            else:
                acc_ref[hh, t] = acc
                m_ref[hh, t] = jnp.broadcast_to(top, (tok, hd))
                l_ref[hh, t] = jnp.broadcast_to(total, (tok, hd))
            return carry

        lax.fori_loop(0, per, own_head, 0)
        if t == GROUP - 1:
            send_out(t)

    def project_prev(j, carry):
        @pl.when(has_prev)
        def _():
            remote(res_send.at[j], res_prev.at[j], next_send.at[j], prev_recv.at[j], base + j).wait_recv()
            remote(sc_send, sc_prev.at[j], next_sc_send.at[j], prev_sc_recv.at[j], base + j).wait_recv()
            scales = jnp.transpose(jnp.broadcast_to(sc_prev[j][0:1], (tok, tok)))
            tile = res_prev[j]
            rows = pl.ds(pl.multiple_of(j * tok, tok), tok)
            for hh in range(per):
                normed = norm_head(tile, scales, hh)
                made = jnp.dot(normed, w_attn[hh][:, hd:], preferred_element_type=F32).astype(BF16)
                k_prev[hh, rows, :] = made[:, :hd]
                v_prev[hh, rows, :] = made[:, hd:]

        @pl.when(jnp.logical_not(has_prev))
        def _():
            rows = pl.ds(pl.multiple_of(j * tok, tok), tok)
            for hh in range(per):
                k_prev[hh, rows, :] = jnp.zeros((tok, hd), BF16)
                v_prev[hh, rows, :] = jnp.zeros((tok, hd), BF16)

        return carry

    lax.fori_loop(0, GROUP, project_prev, 0)

    for t in range(GROUP - 2, -1, -1):
        first = (t + 1) * tok
        count = (GROUP - 1 - t) * tok
        bias = hidden_bias(first, count, (begins[t] - base + GROUP) * tok)

        def prev_head(hh, carry, t=t, first=first, bias=bias):
            q = q_own[hh, t * tok : (t + 1) * tok, :]
            bulk = score(q, k_prev[hh, first:, :]) + bias
            before = m_ref[hh, t][:, 0:1]
            top = jnp.maximum(before, jnp.max(bulk, axis=-1, keepdims=True))
            exps = jnp.exp((bulk - top) * slope)
            fade = jnp.exp((before - top) * slope)
            total = l_ref[hh, t][:, 0:1] * fade + jnp.sum(exps, axis=-1, keepdims=True)
            acc = acc_ref[hh, t] * fade + jnp.dot(
                exps.astype(BF16), v_prev[hh, first:, :], preferred_element_type=F32
            )
            finish(hh, t, acc, total)
            return carry

        lax.fori_loop(0, per, prev_head, 0)
        send_out(t)

    @pl.when(me < ctx - 1)
    def _():
        halo.wait_send()

    def drain(j, carry):
        @pl.when(has_next)
        def _():
            remote(res_send.at[j], res_prev.at[r], next_send.at[j], prev_recv.at[r], base + j).wait_send()
            remote(sc_send, sc_prev.at[r], next_sc_send.at[j], prev_sc_recv.at[r], base + j).wait_send()

        @pl.when(j != r)
        def _():
            remote(res_send.at[j], res_own.at[r], own_send.at[j], own_recv.at[r], base + j).wait_send()
            remote(sc_send, sc_own.at[r], own_sc_send.at[j], own_sc_recv.at[r], base + j).wait_send()
            columns = pl.ds(pl.multiple_of(j * wide, wide), wide)
            sent = remote(out_buf.at[j], out.at[:, columns], out_send.at[j], out_recv.at[j], base + j)
            sent.wait_send()
            sent.wait_recv()

        @pl.when(j == r)
        def _():
            columns = pl.ds(pl.multiple_of(r * wide, wide), wide)
            pltpu.make_async_copy(out_buf.at[j], out.at[:, columns], own_sem.at[1]).wait()

        return carry

    lax.fori_loop(0, GROUP, drain, 0)


def shards(ctx, hidden_in, in_weight, feat_filter, inner_filter, norm_gain, attn_weight, doc_lengths):
    tok, channels = hidden_in.shape
    heads, hd, _ = in_weight.shape
    per = heads // GROUP
    wide = per * hd
    span = GROUP * tok
    any_spec = pl.BlockSpec(memory_space=pl.ANY)
    vmem_spec = pl.BlockSpec(memory_space=pltpu.VMEM)
    dma = pltpu.SemaphoreType.DMA
    return pl.pallas_call(
        functools.partial(kernel, ctx),
        out_shape=jax.ShapeDtypeStruct((tok, channels), BF16),
        in_specs=[
            pl.BlockSpec(memory_space=pltpu.SMEM),
            any_spec,
            any_spec,
            vmem_spec,
            vmem_spec,
            vmem_spec,
            any_spec,
        ],
        out_specs=any_spec,
        scratch_shapes=[
            pltpu.VMEM((HALO + tok, channels), BF16),
            pltpu.VMEM((heads, hd, 3 * hd), BF16),
            pltpu.VMEM((per, hd, 3 * hd), BF16),
            pltpu.VMEM((GROUP, tok, wide), BF16),
            pltpu.VMEM((GROUP, tok, wide), BF16),
            pltpu.VMEM((GROUP, tok, wide), BF16),
            pltpu.VMEM((8, tok), F32),
            pltpu.VMEM((GROUP, 8, tok), F32),
            pltpu.VMEM((GROUP, 8, tok), F32),
            pltpu.VMEM((tok, hd), F32),
            pltpu.VMEM((per, span, hd), BF16),
            pltpu.VMEM((per, span, hd), BF16),
            pltpu.VMEM((per, span, hd), BF16),
            pltpu.VMEM((per, span, hd), BF16),
            pltpu.VMEM((per, span, hd), BF16),
            pltpu.VMEM((per, GROUP, tok, hd), F32),
            pltpu.VMEM((per, GROUP, tok, hd), F32),
            pltpu.VMEM((per, GROUP, tok, hd), F32),
            pltpu.VMEM((GROUP, tok, wide), BF16),
            dma((5,)),
            dma((2,)),
        ]
        + [dma((GROUP,))] * 10
        + [dma((2,))],
        compiler_params=pltpu.CompilerParams(
            collective_id=0, has_side_effects=True, vmem_limit_bytes=56 * 1024 * 1024
        ),
        cost_estimate=pl.CostEstimate(
            flops=6_000_000_000, bytes_accessed=9_000_000, transcendentals=4_200_000
        ),
    )(
        doc_lengths,
        hidden_in,
        in_weight,
        feat_filter,
        inner_filter,
        norm_gain.reshape(1, channels),
        attn_weight,
    )


def solution(mesh):
    return jax.shard_map(
        functools.partial(shards, mesh.shape["ctx"]),
        mesh=mesh,
        in_specs=(P(("groups", "ctx"), None), P(), P(), P(), P(), P(), P("groups")),
        out_specs=P(("groups", "ctx"), None),
        check_vma=False,
    )
```

```python
import functools

import jax
import jax.numpy as jnp
from jax import lax
from jax.experimental import pallas as pl
from jax.experimental.pallas import tpu as pltpu
from jax.sharding import PartitionSpec as P

GROUP = 8
HALO = 16
LAG = 3
MESH = pl.DeviceIdType.MESH
F32 = jnp.float32
BF16 = jnp.bfloat16
NEG = -1e30


def remote(src, dst, send_sem, recv_sem, device):
    return pltpu.make_async_remote_copy(
        src_ref=src,
        dst_ref=dst,
        send_sem=send_sem,
        recv_sem=recv_sem,
        device_id={"ctx": device},
        device_id_type=MESH,
    )


def kernel(
    ctx,
    doc_ref,
    hid,
    in_w,
    feat_ref,
    inner_ref,
    gain_ref,
    attn_w,
    out,
    x_ext,
    w_in,
    w_attn,
    res_send,
    res_own,
    res_prev,
    sc_send,
    sc_own,
    sc_prev,
    ssq,
    q_own,
    k_own,
    v_own,
    k_prev,
    v_prev,
    acc_ref,
    m_ref,
    l_ref,
    out_buf,
    load_sem,
    halo_sem,
    next_send,
    own_send,
    own_recv,
    prev_recv,
    next_sc_send,
    own_sc_send,
    own_sc_recv,
    prev_sc_recv,
    out_send,
    out_recv,
    own_sem,
):
    tok, channels = hid.shape
    hd = w_in.shape[1]
    heads = w_in.shape[0]
    per = heads // GROUP
    wide = per * hd
    taps = feat_ref.shape[0]
    inner_taps = inner_ref.shape[0]
    me = lax.axis_index("ctx")
    r = lax.rem(me, GROUP)
    group = lax.div(me, GROUP)
    base = group * GROUP
    has_prev = group > 0
    has_next = group < ctx // GROUP - 1

    loads = [
        pltpu.make_async_copy(hid, x_ext.at[pl.ds(HALO, tok)], load_sem.at[0]),
        pltpu.make_async_copy(in_w, w_in, load_sem.at[1]),
    ]
    for s in range(3):
        loads.append(
            pltpu.make_async_copy(
                attn_w.at[s, pl.ds(r * per, per)],
                w_attn.at[:, :, pl.ds(s * hd, hd)],
                load_sem.at[2 + s],
            )
        )
    for copy in loads:
        copy.start()

    barrier = pltpu.get_barrier_semaphore()

    def signal_own(j, carry):
        @pl.when(j != r)
        def _():
            pl.semaphore_signal(
                barrier, inc=1, device_id={"ctx": base + j}, device_id_type=MESH
            )

        return carry

    lax.fori_loop(0, GROUP, signal_own, 0)

    @pl.when(has_prev)
    def _():
        pl.semaphore_signal(barrier, inc=1, device_id={"ctx": me - GROUP}, device_id_type=MESH)

    @pl.when(has_prev & (r == 0))
    def _():
        pl.semaphore_signal(barrier, inc=1, device_id={"ctx": me - 1}, device_id_type=MESH)

    hears = jnp.where(has_next, jnp.where(r == GROUP - 1, GROUP + 1, GROUP), GROUP - 1)
    pl.semaphore_wait(barrier, hears)

    halo = remote(
        hid.at[pl.ds(tok - HALO, HALO)],
        x_ext.at[pl.ds(0, HALO)],
        halo_sem.at[0],
        halo_sem.at[1],
        lax.rem(me + 1, ctx),
    )

    @pl.when(me < ctx - 1)
    def _():
        halo.start()

    def doc_step(d, carry):
        end = carry[0] + doc_ref[d]
        return (end,) + tuple(
            jnp.where(end <= block, end, begin)
            for begin, block in zip(carry[1:], [base + t for t in range(GROUP)] + [me])
        )

    zero = jnp.int32(0)
    found = lax.fori_loop(0, doc_ref.shape[0], doc_step, (zero,) * (GROUP + 2))
    begins = found[1 : GROUP + 1]
    my_begin = found[GROUP + 1]

    loads[0].wait()
    loads[1].wait()

    @pl.when(me > 0)
    def _():
        halo.wait_recv()

    @pl.when(me == 0)
    def _():
        x_ext[0:HALO, :] = jnp.zeros((HALO, channels), BF16)

    keep = jnp.where(my_begin < me, 1.0, 0.0).astype(F32)
    x_ext[0:HALO, :] = (x_ext[0:HALO, :].astype(F32) * keep).astype(BF16)

    ssq[...] = jnp.zeros_like(ssq)

    def forward(j, src):
        @pl.when(has_next & (j > 0))
        def _():
            remote(
                src, res_prev.at[j], next_send.at[j], prev_recv.at[j], me + GROUP
            ).start()

    def receive_own(step):
        j = lax.rem(r + 2 * GROUP - 1 - step, GROUP)
        remote(res_send.at[j], res_own.at[j], own_send.at[j], own_recv.at[j], base + j).wait_recv()
        forward(j, res_own.at[j])

    def mix_chunk(step, carry):
        chunk = lax.rem(r + 1 + step, GROUP)
        total = ssq[...]
        for hh in range(per):
            head = chunk * per + hh
            x = x_ext[:, pl.ds(pl.multiple_of(head * hd, hd), hd)]
            streams = jnp.dot(x, w_in[head], preferred_element_type=F32).astype(BF16).astype(F32)
            taps_f = feat_ref[:, pl.ds(pl.multiple_of(head * 3 * hd, 3 * hd), 3 * hd)]
            feats = streams * taps_f[0:1]
            for t in range(1, taps):
                feats = feats + pltpu.roll(streams, t, 0) * taps_f[t : t + 1]
            gated = (feats[:, hd : 2 * hd] * feats[:, 2 * hd :]).astype(BF16).astype(F32)
            taps_i = inner_ref[:, pl.ds(pl.multiple_of(head * hd, hd), hd)]
            conv = gated * taps_i[0:1]
            for t in range(1, inner_taps):
                conv = conv + pltpu.roll(gated, t, 0) * taps_i[t : t + 1]
            residual = (x[HALO:].astype(F32) + feats[HALO:, :hd] * conv[HALO:]).astype(BF16)
            res_send[chunk, :, hh * hd : (hh + 1) * hd] = residual
            res_float = residual.astype(F32)
            total = total + res_float * res_float
        ssq[...] = total

        @pl.when(chunk != r)
        def _():
            remote(
                res_send.at[chunk],
                res_own.at[r],
                own_send.at[chunk],
                own_recv.at[r],
                base + chunk,
            ).start()

        @pl.when(step >= LAG)
        def _():
            receive_own(step - LAG)

        return carry

    lax.fori_loop(0, GROUP, mix_chunk, 0)
    keep_own = pltpu.make_async_copy(res_send.at[r], res_own.at[r], own_sem.at[0])
    keep_own.start()
    forward(r, res_send.at[r])

    mean = jnp.sum(ssq[...], axis=-1, keepdims=True) * (1.0 / channels)
    scale = lax.rsqrt(mean + 1e-05)
    sc_send[...] = jnp.transpose(jnp.broadcast_to(scale, (tok, tok)))[0:8]

    def send_scale(j, carry):
        @pl.when(j != r)
        def _():
            remote(sc_send, sc_own.at[r], own_sc_send.at[j], own_sc_recv.at[r], base + j).start()

        return carry

    lax.fori_loop(0, GROUP, send_scale, 0)
    sc_own[r] = sc_send[...]
    for step in range(GROUP - LAG, GROUP - 1):
        receive_own(step)

    def receive_scale(j, carry):
        @pl.when(j != r)
        def _():
            remote(sc_send, sc_own.at[j], own_sc_send.at[j], own_sc_recv.at[j], base + j).wait_recv()

        return carry

    lax.fori_loop(0, GROUP, receive_scale, 0)
    scales_on = remote(
        sc_own, sc_prev, next_sc_send.at[0], prev_sc_recv.at[0], lax.rem(me + GROUP, ctx)
    )

    @pl.when(has_next)
    def _():
        scales_on.start()

    keep_own.wait()
    for copy in loads[2:]:
        copy.wait()
    gain = gain_ref[:, pl.ds(pl.multiple_of(r * wide, wide), wide)]

    def norm_head(res_tile, scales, hh):
        columns = slice(hh * hd, (hh + 1) * hd)
        return (res_tile[:, columns].astype(F32) * scales * gain[:, columns]).astype(BF16)

    def project_own(j, carry):
        scales = jnp.transpose(jnp.broadcast_to(sc_own[j][0:1], (tok, tok)))
        tile = res_own[j]
        rows = pl.ds(pl.multiple_of(j * tok, tok), tok)
        for hh in range(per):
            normed = norm_head(tile, scales, hh)
            made = jnp.dot(normed, w_attn[hh], preferred_element_type=F32).astype(BF16)
            q_own[hh, rows, :] = made[:, :hd]
            k_own[hh, rows, :] = made[:, hd : 2 * hd]
            v_own[hh, rows, :] = made[:, 2 * hd :]
        return carry

    lax.fori_loop(0, GROUP, project_own, 0)

    slope = hd ** (-0.5)
    contract_last = (((1,), (1,)), ((), ()))

    def score(q, k):
        return lax.dot_general(q, k, contract_last, preferred_element_type=F32)

    def hidden_bias(first, count, begin_row):
        columns = first + lax.broadcasted_iota(jnp.int32, (1, count), 1)
        return jnp.where(columns >= begin_row, 0.0, NEG).astype(F32)

    def finish(hh, t, acc, total):
        columns = pl.ds(pl.multiple_of(hh * hd, hd), hd)
        res_float = res_own[t, :, columns].astype(F32)
        out_buf[t, :, columns] = (res_float + acc * (1.0 / total)).astype(BF16)

    def send_out(t):
        columns = pl.ds(pl.multiple_of(r * wide, wide), wide)

        @pl.when(r != t)
        def _():
            remote(
                out_buf.at[t], out.at[:, columns], out_send.at[t], out_recv.at[r], base + t
            ).start()

        @pl.when(r == t)
        def _():
            pltpu.make_async_copy(out_buf.at[t], out.at[:, columns], own_sem.at[1]).start()

    tri = lax.broadcasted_iota(jnp.int32, (tok, tok), 0) >= lax.broadcasted_iota(
        jnp.int32, (tok, tok), 1
    )

    for t in range(GROUP - 1, -1, -1):
        bias = hidden_bias(0, t * tok, (begins[t] - base) * tok) if t else None

        def own_head(hh, carry, t=t, bias=bias):
            q = q_own[hh, t * tok : (t + 1) * tok, :]
            diag = jnp.where(tri, score(q, k_own[hh, t * tok : (t + 1) * tok, :]), NEG)
            top = jnp.max(diag, axis=-1, keepdims=True)
            if t:
                bulk = score(q, k_own[hh, : t * tok, :]) + bias
                top = jnp.maximum(top, jnp.max(bulk, axis=-1, keepdims=True))
            exps = jnp.exp((diag - top) * slope)
            total = jnp.sum(exps, axis=-1, keepdims=True)
            acc = jnp.dot(
                exps.astype(BF16), v_own[hh, t * tok : (t + 1) * tok, :], preferred_element_type=F32
            )
            if t:
                exps = jnp.exp((bulk - top) * slope)
                total = total + jnp.sum(exps, axis=-1, keepdims=True)
                acc = acc + jnp.dot(
                    exps.astype(BF16), v_own[hh, : t * tok, :], preferred_element_type=F32
                )
            if t == GROUP - 1:
                finish(hh, t, acc, total)
            else:
                acc_ref[hh, t] = acc
                m_ref[hh, t] = jnp.broadcast_to(top, (tok, hd))
                l_ref[hh, t] = jnp.broadcast_to(total, (tok, hd))
            return carry

        lax.fori_loop(0, per, own_head, 0)
        if t == GROUP - 1:
            send_out(t)

    def project_prev(j, carry):
        @pl.when(has_prev)
        def _():
            remote(res_own.at[j], res_prev.at[j], next_send.at[j], prev_recv.at[j], me).wait_recv()
            scales = jnp.transpose(jnp.broadcast_to(sc_prev[j][0:1], (tok, tok)))
            tile = res_prev[j]
            rows = pl.ds(pl.multiple_of(j * tok, tok), tok)
            for hh in range(per):
                normed = norm_head(tile, scales, hh)
                made = jnp.dot(normed, w_attn[hh][:, hd:], preferred_element_type=F32).astype(BF16)
                k_prev[hh, rows, :] = made[:, :hd]
                v_prev[hh, rows, :] = made[:, hd:]

        @pl.when(jnp.logical_not(has_prev))
        def _():
            rows = pl.ds(pl.multiple_of(j * tok, tok), tok)
            for hh in range(per):
                k_prev[hh, rows, :] = jnp.zeros((tok, hd), BF16)
                v_prev[hh, rows, :] = jnp.zeros((tok, hd), BF16)

        return carry

    @pl.when(has_prev)
    def _():
        scales_on.wait_recv()

    lax.fori_loop(1, GROUP, project_prev, 0)

    def attend_prev(t):
        first = (t + 1) * tok
        count = (GROUP - 1 - t) * tok
        bias = hidden_bias(first, count, (begins[t] - base + GROUP) * tok)

        def prev_head(hh, carry, t=t, first=first, bias=bias):
            q = q_own[hh, t * tok : (t + 1) * tok, :]
            bulk = score(q, k_prev[hh, first:, :]) + bias
            before = m_ref[hh, t][:, 0:1]
            top = jnp.maximum(before, jnp.max(bulk, axis=-1, keepdims=True))
            exps = jnp.exp((bulk - top) * slope)
            fade = jnp.exp((before - top) * slope)
            total = l_ref[hh, t][:, 0:1] * fade + jnp.sum(exps, axis=-1, keepdims=True)
            acc = acc_ref[hh, t] * fade + jnp.dot(
                exps.astype(BF16), v_prev[hh, first:, :], preferred_element_type=F32
            )
            finish(hh, t, acc, total)
            return carry

        lax.fori_loop(0, per, prev_head, 0)

    def attend_step(step, carry):
        tile = lax.rem(r + 1 + step, GROUP)
        for t in range(GROUP - 1):
            pl.when(tile == t)(functools.partial(attend_prev, t))

        @pl.when(tile < GROUP - 1)
        def _():
            send_out(tile)

        return carry

    lax.fori_loop(0, GROUP, attend_step, 0)

    @pl.when(me < ctx - 1)
    def _():
        halo.wait_send()

    @pl.when(has_next)
    def _():
        scales_on.wait_send()

    def drain(j, carry):
        @pl.when(has_next & (j > 0))
        def _():
            remote(res_own.at[j], res_prev.at[j], next_send.at[j], prev_recv.at[j], me).wait_send()

        @pl.when(j != r)
        def _():
            remote(res_send.at[j], res_own.at[r], own_send.at[j], own_recv.at[r], base + j).wait_send()
            remote(sc_send, sc_own.at[r], own_sc_send.at[j], own_sc_recv.at[r], base + j).wait_send()
            columns = pl.ds(pl.multiple_of(j * wide, wide), wide)
            sent = remote(out_buf.at[j], out.at[:, columns], out_send.at[j], out_recv.at[j], base + j)
            sent.wait_send()
            sent.wait_recv()

        @pl.when(j == r)
        def _():
            columns = pl.ds(pl.multiple_of(r * wide, wide), wide)
            pltpu.make_async_copy(out_buf.at[j], out.at[:, columns], own_sem.at[1]).wait()

        return carry

    lax.fori_loop(0, GROUP, drain, 0)


def shards(ctx, hidden_in, in_weight, feat_filter, inner_filter, norm_gain, attn_weight, doc_lengths):
    tok, channels = hidden_in.shape
    heads, hd, _ = in_weight.shape
    per = heads // GROUP
    wide = per * hd
    span = GROUP * tok
    any_spec = pl.BlockSpec(memory_space=pl.ANY)
    vmem_spec = pl.BlockSpec(memory_space=pltpu.VMEM)
    dma = pltpu.SemaphoreType.DMA
    return pl.pallas_call(
        functools.partial(kernel, ctx),
        out_shape=jax.ShapeDtypeStruct((tok, channels), BF16),
        in_specs=[
            pl.BlockSpec(memory_space=pltpu.SMEM),
            any_spec,
            any_spec,
            vmem_spec,
            vmem_spec,
            vmem_spec,
            any_spec,
        ],
        out_specs=any_spec,
        scratch_shapes=[
            pltpu.VMEM((HALO + tok, channels), BF16),
            pltpu.VMEM((heads, hd, 3 * hd), BF16),
            pltpu.VMEM((per, hd, 3 * hd), BF16),
            pltpu.VMEM((GROUP, tok, wide), BF16),
            pltpu.VMEM((GROUP, tok, wide), BF16),
            pltpu.VMEM((GROUP, tok, wide), BF16),
            pltpu.VMEM((8, tok), F32),
            pltpu.VMEM((GROUP, 8, tok), F32),
            pltpu.VMEM((GROUP, 8, tok), F32),
            pltpu.VMEM((tok, hd), F32),
            pltpu.VMEM((per, span, hd), BF16),
            pltpu.VMEM((per, span, hd), BF16),
            pltpu.VMEM((per, span, hd), BF16),
            pltpu.VMEM((per, span, hd), BF16),
            pltpu.VMEM((per, span, hd), BF16),
            pltpu.VMEM((per, GROUP, tok, hd), F32),
            pltpu.VMEM((per, GROUP, tok, hd), F32),
            pltpu.VMEM((per, GROUP, tok, hd), F32),
            pltpu.VMEM((GROUP, tok, wide), BF16),
            dma((5,)),
            dma((2,)),
        ]
        + [dma((GROUP,))] * 10
        + [dma((2,))],
        compiler_params=pltpu.CompilerParams(
            collective_id=0, has_side_effects=True, vmem_limit_bytes=56 * 1024 * 1024
        ),
        cost_estimate=pl.CostEstimate(
            flops=6_000_000_000, bytes_accessed=9_000_000, transcendentals=4_200_000
        ),
    )(
        doc_lengths,
        hidden_in,
        in_weight,
        feat_filter,
        inner_filter,
        norm_gain.reshape(1, channels),
        attn_weight,
    )


def solution(mesh):
    return jax.shard_map(
        functools.partial(shards, mesh.shape["ctx"]),
        mesh=mesh,
        in_specs=(P(("groups", "ctx"), None), P(), P(), P(), P(), P(), P("groups")),
        out_specs=P(("groups", "ctx"), None),
        check_vma=False,
    )
```

```python
import functools

import jax
import jax.numpy as jnp
from jax import lax
from jax.experimental import pallas as pl
from jax.experimental.pallas import tpu as pltpu
from jax.sharding import PartitionSpec as P

GROUP = 8
HALO = 16
LAG = 3
MESH = pl.DeviceIdType.MESH
F32 = jnp.float32
BF16 = jnp.bfloat16
NEG = -1e30
LOG2_E = 1.4426950408889634


def remote(src, dst, send_sem, recv_sem, device):
    return pltpu.make_async_remote_copy(
        src_ref=src,
        dst_ref=dst,
        send_sem=send_sem,
        recv_sem=recv_sem,
        device_id={"ctx": device},
        device_id_type=MESH,
    )


def kernel(
    ctx,
    doc_ref,
    hid,
    in_w,
    feat_hbm,
    inner_hbm,
    gain_hbm,
    attn_w,
    out,
    x_ext,
    feat_ref,
    inner_ref,
    gain_ref,
    w_in,
    w_attn,
    res_send,
    res_own,
    res_prev,
    sc_send,
    sc_own,
    sc_prev,
    ssq,
    q_own,
    k_own,
    v_own,
    k_prev,
    v_prev,
    out_buf,
    load_sem,
    halo_sem,
    next_send,
    own_send,
    own_recv,
    prev_recv,
    next_sc_send,
    own_sc_send,
    own_sc_recv,
    prev_sc_recv,
    out_send,
    out_recv,
    own_sem,
):
    tok, channels = hid.shape
    hd = w_in.shape[1]
    heads = w_in.shape[0]
    per = heads // GROUP
    wide = per * hd
    taps = feat_ref.shape[0]
    inner_taps = inner_ref.shape[0]
    me = lax.axis_index("ctx")
    r = lax.rem(me, GROUP)
    group = lax.div(me, GROUP)
    base = group * GROUP
    has_prev = group > 0
    has_next = group < ctx // GROUP - 1

    loads = [
        pltpu.make_async_copy(hid, x_ext.at[pl.ds(HALO, tok)], load_sem.at[0]),
        pltpu.make_async_copy(in_w, w_in, load_sem.at[1]),
    ]
    for s in range(3):
        loads.append(
            pltpu.make_async_copy(
                attn_w.at[s, pl.ds(r * per, per)],
                w_attn.at[:, :, pl.ds(s * hd, hd)],
                load_sem.at[2 + s],
            )
        )
    loads += [
        pltpu.make_async_copy(feat_hbm, feat_ref, load_sem.at[5]),
        pltpu.make_async_copy(inner_hbm, inner_ref, load_sem.at[6]),
        pltpu.make_async_copy(gain_hbm, gain_ref, load_sem.at[7]),
    ]
    for copy in loads:
        copy.start()

    barrier = pltpu.get_barrier_semaphore()

    def signal_own(j, carry):
        @pl.when(j != r)
        def _():
            pl.semaphore_signal(
                barrier, inc=1, device_id={"ctx": base + j}, device_id_type=MESH
            )

        return carry

    lax.fori_loop(0, GROUP, signal_own, 0)

    @pl.when(has_prev)
    def _():
        pl.semaphore_signal(barrier, inc=1, device_id={"ctx": me - GROUP}, device_id_type=MESH)

    @pl.when(has_prev & (r == 0))
    def _():
        pl.semaphore_signal(barrier, inc=1, device_id={"ctx": me - 1}, device_id_type=MESH)

    hears = jnp.where(has_next, jnp.where(r == GROUP - 1, GROUP + 1, GROUP), GROUP - 1)
    pl.semaphore_wait(barrier, hears)

    halo = remote(
        hid.at[pl.ds(tok - HALO, HALO)],
        x_ext.at[pl.ds(0, HALO)],
        halo_sem.at[0],
        halo_sem.at[1],
        lax.rem(me + 1, ctx),
    )

    @pl.when(me < ctx - 1)
    def _():
        halo.start()

    def doc_step(d, carry):
        end = carry[0] + doc_ref[d]
        return (end,) + tuple(
            jnp.where(end <= block, end, begin)
            for begin, block in zip(carry[1:], [base + t for t in range(GROUP)] + [me])
        )

    zero = jnp.int32(0)
    found = lax.fori_loop(0, doc_ref.shape[0], doc_step, (zero,) * (GROUP + 2))
    begins = found[1 : GROUP + 1]
    my_begin = found[GROUP + 1]

    loads[0].wait()
    loads[1].wait()
    loads[5].wait()
    loads[6].wait()

    @pl.when(me > 0)
    def _():
        halo.wait_recv()

    @pl.when(me == 0)
    def _():
        x_ext[0:HALO, :] = jnp.zeros((HALO, channels), BF16)

    keep = jnp.where(my_begin < me, 1.0, 0.0).astype(F32)
    x_ext[0:HALO, :] = (x_ext[0:HALO, :].astype(F32) * keep).astype(BF16)

    ssq[...] = jnp.zeros_like(ssq)

    def forward(j, src):
        @pl.when(has_next & (j > 0))
        def _():
            remote(
                src, res_prev.at[j], next_send.at[j], prev_recv.at[j], me + GROUP
            ).start()

    def receive_own(step):
        j = lax.rem(r + 2 * GROUP - 1 - step, GROUP)
        remote(res_send.at[j], res_own.at[j], own_send.at[j], own_recv.at[j], base + j).wait_recv()
        forward(j, res_own.at[j])

    def mix_chunk(step, carry):
        chunk = lax.rem(r + 1 + step, GROUP)
        total = ssq[...]
        for hh in range(per):
            head = chunk * per + hh
            x = x_ext[:, pl.ds(pl.multiple_of(head * hd, hd), hd)]
            streams = jnp.dot(x, w_in[head], preferred_element_type=F32).astype(BF16).astype(F32)
            taps_f = feat_ref[:, pl.ds(pl.multiple_of(head * 3 * hd, 3 * hd), 3 * hd)]
            feats = streams * taps_f[0:1]
            for t in range(1, taps):
                feats = feats + pltpu.roll(streams, t, 0) * taps_f[t : t + 1]
            gated = (feats[:, hd : 2 * hd] * feats[:, 2 * hd :]).astype(BF16).astype(F32)
            taps_i = inner_ref[:, pl.ds(pl.multiple_of(head * hd, hd), hd)]
            conv = gated * taps_i[0:1]
            for t in range(1, inner_taps):
                conv = conv + pltpu.roll(gated, t, 0) * taps_i[t : t + 1]
            residual = (x[HALO:].astype(F32) + feats[HALO:, :hd] * conv[HALO:]).astype(BF16)
            res_send[chunk, :, hh * hd : (hh + 1) * hd] = residual
            res_float = residual.astype(F32)
            total = total + res_float * res_float
        ssq[...] = total

        @pl.when(chunk != r)
        def _():
            remote(
                res_send.at[chunk],
                res_own.at[r],
                own_send.at[chunk],
                own_recv.at[r],
                base + chunk,
            ).start()

        @pl.when(step >= LAG)
        def _():
            receive_own(step - LAG)

        return carry

    lax.fori_loop(0, GROUP, mix_chunk, 0)
    keep_own = pltpu.make_async_copy(res_send.at[r], res_own.at[r], own_sem.at[0])
    keep_own.start()
    forward(r, res_send.at[r])

    mean = jnp.sum(ssq[...], axis=-1, keepdims=True) * (1.0 / channels)
    scale = lax.rsqrt(mean + 1e-05)
    sc_send[...] = jnp.transpose(jnp.broadcast_to(scale, (tok, tok)))[0:8]

    def send_scale(j, carry):
        @pl.when(j != r)
        def _():
            remote(sc_send, sc_own.at[r], own_sc_send.at[j], own_sc_recv.at[r], base + j).start()

        return carry

    lax.fori_loop(0, GROUP, send_scale, 0)
    sc_own[r] = sc_send[...]
    for step in range(GROUP - LAG, GROUP - 1):
        receive_own(step)

    def receive_scale(j, carry):
        @pl.when(j != r)
        def _():
            remote(sc_send, sc_own.at[j], own_sc_send.at[j], own_sc_recv.at[j], base + j).wait_recv()

        return carry

    lax.fori_loop(0, GROUP, receive_scale, 0)
    scales_on = remote(
        sc_own, sc_prev, next_sc_send.at[0], prev_sc_recv.at[0], lax.rem(me + GROUP, ctx)
    )

    @pl.when(has_next)
    def _():
        scales_on.start()

    keep_own.wait()
    for copy in loads[2:5] + loads[7:]:
        copy.wait()
    gain = gain_ref[:, pl.ds(pl.multiple_of(r * wide, wide), wide)]

    def norm_head(res_tile, scales, hh):
        columns = slice(hh * hd, (hh + 1) * hd)
        return (res_tile[:, columns].astype(F32) * scales * gain[:, columns]).astype(BF16)

    def project_own(j, carry):
        scales = jnp.transpose(jnp.broadcast_to(sc_own[j][0:1], (tok, tok)))
        tile = res_own[j]
        rows = pl.ds(pl.multiple_of(j * tok, tok), tok)
        for hh in range(per):
            normed = norm_head(tile, scales, hh)
            made = jnp.dot(normed, w_attn[hh], preferred_element_type=F32).astype(BF16)
            q_own[hh, rows, :] = made[:, :hd]
            k_own[hh, rows, :] = made[:, hd : 2 * hd]
            v_own[hh, rows, :] = made[:, 2 * hd :]
        return carry

    lax.fori_loop(0, GROUP, project_own, 0)

    slope = hd ** (-0.5) * LOG2_E
    contract_last = (((1,), (1,)), ((), ()))

    def score(q, k):
        return lax.dot_general(q, k, contract_last, preferred_element_type=F32)

    def hidden_bias(first, count, begin_row):
        columns = first + lax.broadcasted_iota(jnp.int32, (1, count), 1)
        return jnp.where(columns >= begin_row, 0.0, NEG).astype(F32)

    def finish(hh, t, acc, total):
        columns = pl.ds(pl.multiple_of(hh * hd, hd), hd)
        res_float = res_own[t, :, columns].astype(F32)
        out_buf[t, :, columns] = (res_float + acc * (1.0 / total)).astype(BF16)

    def send_out(t):
        columns = pl.ds(pl.multiple_of(r * wide, wide), wide)

        @pl.when(r != t)
        def _():
            remote(
                out_buf.at[t], out.at[:, columns], out_send.at[t], out_recv.at[r], base + t
            ).start()

        @pl.when(r == t)
        def _():
            pltpu.make_async_copy(out_buf.at[t], out.at[:, columns], own_sem.at[1]).start()

    tri = lax.broadcasted_iota(jnp.int32, (tok, tok), 0) >= lax.broadcasted_iota(
        jnp.int32, (tok, tok), 1
    )

    def project_prev(j, carry):
        @pl.when(has_prev)
        def _():
            remote(res_own.at[j], res_prev.at[j], next_send.at[j], prev_recv.at[j], me).wait_recv()
            scales = jnp.transpose(jnp.broadcast_to(sc_prev[j][0:1], (tok, tok)))
            tile = res_prev[j]
            rows = pl.ds(pl.multiple_of(j * tok, tok), tok)
            for hh in range(per):
                normed = norm_head(tile, scales, hh)
                made = jnp.dot(normed, w_attn[hh][:, hd:], preferred_element_type=F32).astype(BF16)
                k_prev[hh, rows, :] = made[:, :hd]
                v_prev[hh, rows, :] = made[:, hd:]

        @pl.when(jnp.logical_not(has_prev))
        def _():
            rows = pl.ds(pl.multiple_of(j * tok, tok), tok)
            for hh in range(per):
                k_prev[hh, rows, :] = jnp.zeros((tok, hd), BF16)
                v_prev[hh, rows, :] = jnp.zeros((tok, hd), BF16)

        return carry

    @pl.when(has_prev)
    def _():
        scales_on.wait_recv()

    lax.fori_loop(1, GROUP, project_prev, 0)

    def attend(t):
        own = slice(t * tok, (t + 1) * tok)
        first = (t + 1) * tok
        bias_own = hidden_bias(0, t * tok, (begins[t] - base) * tok) if t else None
        bias_prev = (
            hidden_bias(first, (GROUP - 1 - t) * tok, (begins[t] - base + GROUP) * tok)
            if t < GROUP - 1
            else None
        )

        def one_head(hh, carry):
            q = q_own[hh, own, :]
            parts = [(jnp.where(tri, score(q, k_own[hh, own, :]), NEG), v_own[hh, own, :])]
            if t:
                parts.append((score(q, k_own[hh, : t * tok, :]) + bias_own, v_own[hh, : t * tok, :]))
            if t < GROUP - 1:
                parts.append((score(q, k_prev[hh, first:, :]) + bias_prev, v_prev[hh, first:, :]))
            top = functools.reduce(
                jnp.maximum, [jnp.max(part, axis=-1, keepdims=True) for part, _ in parts]
            )
            total = 0.0
            acc = 0.0
            for part, values in parts:
                exps = jnp.exp2((part - top) * slope)
                total = total + jnp.sum(exps, axis=-1, keepdims=True)
                acc = acc + jnp.dot(exps.astype(BF16), values, preferred_element_type=F32)
            finish(hh, t, acc, total)
            return carry

        lax.fori_loop(0, per, one_head, 0, unroll=True)

    def attend_step(step, carry):
        tile = lax.rem(r + 1 + step, GROUP)
        for t in range(GROUP):
            pl.when(tile == t)(functools.partial(attend, t))
        send_out(tile)
        return carry

    lax.fori_loop(0, GROUP, attend_step, 0)

    @pl.when(me < ctx - 1)
    def _():
        halo.wait_send()

    @pl.when(has_next)
    def _():
        scales_on.wait_send()

    def drain(j, carry):
        @pl.when(has_next & (j > 0))
        def _():
            remote(res_own.at[j], res_prev.at[j], next_send.at[j], prev_recv.at[j], me).wait_send()

        @pl.when(j != r)
        def _():
            remote(res_send.at[j], res_own.at[r], own_send.at[j], own_recv.at[r], base + j).wait_send()
            remote(sc_send, sc_own.at[r], own_sc_send.at[j], own_sc_recv.at[r], base + j).wait_send()
            columns = pl.ds(pl.multiple_of(j * wide, wide), wide)
            sent = remote(out_buf.at[j], out.at[:, columns], out_send.at[j], out_recv.at[j], base + j)
            sent.wait_send()
            sent.wait_recv()

        @pl.when(j == r)
        def _():
            columns = pl.ds(pl.multiple_of(r * wide, wide), wide)
            pltpu.make_async_copy(out_buf.at[j], out.at[:, columns], own_sem.at[1]).wait()

        return carry

    lax.fori_loop(0, GROUP, drain, 0)


def shards(ctx, hidden_in, in_weight, feat_filter, inner_filter, norm_gain, attn_weight, doc_lengths):
    tok, channels = hidden_in.shape
    heads, hd, _ = in_weight.shape
    per = heads // GROUP
    wide = per * hd
    span = GROUP * tok
    any_spec = pl.BlockSpec(memory_space=pl.ANY)
    dma = pltpu.SemaphoreType.DMA
    return pl.pallas_call(
        functools.partial(kernel, ctx),
        out_shape=jax.ShapeDtypeStruct((tok, channels), BF16),
        in_specs=[
            pl.BlockSpec(memory_space=pltpu.SMEM),
            any_spec,
            any_spec,
            any_spec,
            any_spec,
            any_spec,
            any_spec,
        ],
        out_specs=any_spec,
        scratch_shapes=[
            pltpu.VMEM((HALO + tok, channels), BF16),
            pltpu.VMEM(feat_filter.shape, F32),
            pltpu.VMEM(inner_filter.shape, F32),
            pltpu.VMEM((1, channels), F32),
            pltpu.VMEM((heads, hd, 3 * hd), BF16),
            pltpu.VMEM((per, hd, 3 * hd), BF16),
            pltpu.VMEM((GROUP, tok, wide), BF16),
            pltpu.VMEM((GROUP, tok, wide), BF16),
            pltpu.VMEM((GROUP, tok, wide), BF16),
            pltpu.VMEM((8, tok), F32),
            pltpu.VMEM((GROUP, 8, tok), F32),
            pltpu.VMEM((GROUP, 8, tok), F32),
            pltpu.VMEM((tok, hd), F32),
            pltpu.VMEM((per, span, hd), BF16),
            pltpu.VMEM((per, span, hd), BF16),
            pltpu.VMEM((per, span, hd), BF16),
            pltpu.VMEM((per, span, hd), BF16),
            pltpu.VMEM((per, span, hd), BF16),
            pltpu.VMEM((GROUP, tok, wide), BF16),
            dma((8,)),
            dma((2,)),
        ]
        + [dma((GROUP,))] * 10
        + [dma((2,))],
        compiler_params=pltpu.CompilerParams(
            collective_id=0, has_side_effects=True, vmem_limit_bytes=56 * 1024 * 1024
        ),
        cost_estimate=pl.CostEstimate(
            flops=6_000_000_000, bytes_accessed=9_000_000, transcendentals=4_200_000
        ),
    )(
        doc_lengths,
        hidden_in,
        in_weight,
        feat_filter,
        inner_filter,
        norm_gain.reshape(1, channels),
        attn_weight,
    )


def solution(mesh):
    return jax.shard_map(
        functools.partial(shards, mesh.shape["ctx"]),
        mesh=mesh,
        in_specs=(P(("groups", "ctx"), None), P(), P(), P(), P(), P(), P("groups")),
        out_specs=P(("groups", "ctx"), None),
        check_vma=False,
    )
```

```python
import functools

import jax
import jax.numpy as jnp
from jax import lax
from jax.experimental import pallas as pl
from jax.experimental.pallas import tpu as pltpu
from jax.sharding import PartitionSpec as P

GROUP = 8
HALO = 16
LAG = 3
MESH = pl.DeviceIdType.MESH
F32 = jnp.float32
BF16 = jnp.bfloat16
NEG = -1e30
LOG2_E = 1.4426950408889634


def remote(src, dst, send_sem, recv_sem, device):
    return pltpu.make_async_remote_copy(
        src_ref=src,
        dst_ref=dst,
        send_sem=send_sem,
        recv_sem=recv_sem,
        device_id={"ctx": device},
        device_id_type=MESH,
    )


def kernel(
    ctx,
    doc_ref,
    hid,
    in_w,
    feat_hbm,
    inner_hbm,
    gain_hbm,
    attn_w,
    out,
    x_ext,
    feat_ref,
    inner_ref,
    gain_ref,
    w_in,
    w_attn,
    res_send,
    res_own,
    res_prev,
    sc_send,
    sc_own,
    sc_prev,
    ssq,
    q_own,
    k_own,
    v_own,
    k_prev,
    v_prev,
    out_buf,
    load_sem,
    halo_sem,
    next_send,
    own_send,
    own_recv,
    prev_recv,
    next_sc_send,
    own_sc_send,
    own_sc_recv,
    prev_sc_recv,
    out_send,
    out_recv,
    own_sem,
):
    tok, channels = hid.shape
    hd = w_in.shape[1]
    heads = w_in.shape[0]
    per = heads // GROUP
    wide = per * hd
    taps = feat_ref.shape[0]
    inner_taps = inner_ref.shape[0]
    me = lax.axis_index("ctx")
    r = lax.rem(me, GROUP)
    group = lax.div(me, GROUP)
    base = group * GROUP
    has_prev = group > 0
    has_next = group < ctx // GROUP - 1

    loads = [
        pltpu.make_async_copy(hid, x_ext.at[pl.ds(HALO, tok)], load_sem.at[0]),
        pltpu.make_async_copy(in_w, w_in, load_sem.at[1]),
    ]
    for s in range(3):
        loads.append(
            pltpu.make_async_copy(
                attn_w.at[s, pl.ds(r * per, per)],
                w_attn.at[:, :, pl.ds(s * hd, hd)],
                load_sem.at[2 + s],
            )
        )
    loads += [
        pltpu.make_async_copy(feat_hbm, feat_ref, load_sem.at[5]),
        pltpu.make_async_copy(inner_hbm, inner_ref, load_sem.at[6]),
        pltpu.make_async_copy(gain_hbm, gain_ref, load_sem.at[7]),
    ]
    for copy in loads:
        copy.start()

    barrier = pltpu.get_barrier_semaphore()

    def signal_own(j, carry):
        @pl.when(j != r)
        def _():
            pl.semaphore_signal(
                barrier, inc=1, device_id={"ctx": base + j}, device_id_type=MESH
            )

        return carry

    lax.fori_loop(0, GROUP, signal_own, 0)

    @pl.when(has_prev)
    def _():
        pl.semaphore_signal(barrier, inc=1, device_id={"ctx": me - GROUP}, device_id_type=MESH)

    @pl.when(has_prev & (r == 0))
    def _():
        pl.semaphore_signal(barrier, inc=1, device_id={"ctx": me - 1}, device_id_type=MESH)

    hears = jnp.where(has_next, jnp.where(r == GROUP - 1, GROUP + 1, GROUP), GROUP - 1)
    pl.semaphore_wait(barrier, hears)

    halo = remote(
        hid.at[pl.ds(tok - HALO, HALO)],
        x_ext.at[pl.ds(0, HALO)],
        halo_sem.at[0],
        halo_sem.at[1],
        lax.rem(me + 1, ctx),
    )

    @pl.when(me < ctx - 1)
    def _():
        halo.start()

    def doc_step(d, carry):
        end = carry[0] + doc_ref[d]
        return (end,) + tuple(
            jnp.where(end <= block, end, begin)
            for begin, block in zip(carry[1:], [base + t for t in range(GROUP)] + [me])
        )

    zero = jnp.int32(0)
    found = lax.fori_loop(0, doc_ref.shape[0], doc_step, (zero,) * (GROUP + 2))
    begins = found[1 : GROUP + 1]
    my_begin = found[GROUP + 1]

    loads[0].wait()
    loads[1].wait()
    loads[5].wait()
    loads[6].wait()

    @pl.when(me > 0)
    def _():
        halo.wait_recv()

    @pl.when(me == 0)
    def _():
        x_ext[0:HALO, :] = jnp.zeros((HALO, channels), BF16)

    keep = jnp.where(my_begin < me, 1.0, 0.0).astype(F32)
    x_ext[0:HALO, :] = (x_ext[0:HALO, :].astype(F32) * keep).astype(BF16)

    ssq[...] = jnp.zeros_like(ssq)

    def forward(j, src):
        @pl.when(has_next & (j > 0))
        def _():
            remote(
                src, res_prev.at[j], next_send.at[j], prev_recv.at[j], me + GROUP
            ).start()

    def receive_own(step):
        j = lax.rem(r + 2 * GROUP - 1 - step, GROUP)
        remote(res_send.at[j], res_own.at[j], own_send.at[j], own_recv.at[j], base + j).wait_recv()
        forward(j, res_own.at[j])

    def mix_chunk(step, carry):
        chunk = lax.rem(r + 1 + step, GROUP)
        total = ssq[...]
        for hh in range(per):
            head = chunk * per + hh
            x = x_ext[:, pl.ds(pl.multiple_of(head * hd, hd), hd)]
            streams = jnp.dot(x, w_in[head], preferred_element_type=F32).astype(BF16).astype(F32)
            taps_f = feat_ref[:, pl.ds(pl.multiple_of(head * 3 * hd, 3 * hd), 3 * hd)]
            feats = streams * taps_f[0:1]
            for t in range(1, taps):
                feats = feats + pltpu.roll(streams, t, 0) * taps_f[t : t + 1]
            gated = (feats[:, hd : 2 * hd] * feats[:, 2 * hd :]).astype(BF16).astype(F32)
            taps_i = inner_ref[:, pl.ds(pl.multiple_of(head * hd, hd), hd)]
            conv = gated * taps_i[0:1]
            for t in range(1, inner_taps):
                conv = conv + pltpu.roll(gated, t, 0) * taps_i[t : t + 1]
            residual = (x[HALO:].astype(F32) + feats[HALO:, :hd] * conv[HALO:]).astype(BF16)
            res_send[chunk, :, hh * hd : (hh + 1) * hd] = residual
            res_float = residual.astype(F32)
            total = total + res_float * res_float
        ssq[...] = total

        @pl.when(chunk != r)
        def _():
            remote(
                res_send.at[chunk],
                res_own.at[r],
                own_send.at[chunk],
                own_recv.at[r],
                base + chunk,
            ).start()

        @pl.when(step >= LAG)
        def _():
            receive_own(step - LAG)

        return carry

    lax.fori_loop(0, GROUP, mix_chunk, 0)
    keep_own = pltpu.make_async_copy(res_send.at[r], res_own.at[r], own_sem.at[0])
    keep_own.start()
    forward(r, res_send.at[r])

    mean = jnp.sum(ssq[...], axis=-1, keepdims=True) * (1.0 / channels)
    scale = lax.rsqrt(mean + 1e-05)
    sc_send[...] = jnp.transpose(jnp.broadcast_to(scale, (tok, tok)))[0:8]

    def send_scale(j, carry):
        @pl.when(j != r)
        def _():
            remote(sc_send, sc_own.at[r], own_sc_send.at[j], own_sc_recv.at[r], base + j).start()

        return carry

    lax.fori_loop(0, GROUP, send_scale, 0)
    sc_own[r] = sc_send[...]
    for step in range(GROUP - LAG, GROUP - 1):
        receive_own(step)

    def receive_scale(j, carry):
        @pl.when(j != r)
        def _():
            remote(sc_send, sc_own.at[j], own_sc_send.at[j], own_sc_recv.at[j], base + j).wait_recv()

        return carry

    lax.fori_loop(0, GROUP, receive_scale, 0)
    scales_on = remote(
        sc_own, sc_prev, next_sc_send.at[0], prev_sc_recv.at[0], lax.rem(me + GROUP, ctx)
    )

    @pl.when(has_next)
    def _():
        scales_on.start()

    keep_own.wait()
    for copy in loads[2:5] + loads[7:]:
        copy.wait()
    gain = gain_ref[:, pl.ds(pl.multiple_of(r * wide, wide), wide)]

    def norm_head(res_tile, scales, hh):
        columns = slice(hh * hd, (hh + 1) * hd)
        return (res_tile[:, columns].astype(F32) * scales * gain[:, columns]).astype(BF16)

    def project_own(j, carry):
        scales = jnp.transpose(jnp.broadcast_to(sc_own[j][0:1], (tok, tok)))
        tile = res_own[j]
        rows = pl.ds(pl.multiple_of(j * tok, tok), tok)
        for hh in range(per):
            normed = norm_head(tile, scales, hh)
            made = jnp.dot(normed, w_attn[hh], preferred_element_type=F32).astype(BF16)
            q_own[hh, rows, :] = made[:, :hd]
            k_own[hh, rows, :] = made[:, hd : 2 * hd]
            v_own[hh, rows, :] = made[:, 2 * hd :]
        return carry

    lax.fori_loop(0, GROUP, project_own, 0, unroll=4)

    slope = hd ** (-0.5) * LOG2_E
    contract_last = (((1,), (1,)), ((), ()))

    def score(q, k):
        return lax.dot_general(q, k, contract_last, preferred_element_type=F32)

    def hidden_bias(first, count, begin_row):
        columns = first + lax.broadcasted_iota(jnp.int32, (1, count), 1)
        return jnp.where(columns >= begin_row, 0.0, NEG).astype(F32)

    def finish(hh, t, acc, total):
        columns = pl.ds(pl.multiple_of(hh * hd, hd), hd)
        res_float = res_own[t, :, columns].astype(F32)
        out_buf[t, :, columns] = (res_float + acc * (1.0 / total)).astype(BF16)

    def send_out(t):
        columns = pl.ds(pl.multiple_of(r * wide, wide), wide)

        @pl.when(r != t)
        def _():
            remote(
                out_buf.at[t], out.at[:, columns], out_send.at[t], out_recv.at[r], base + t
            ).start()

        @pl.when(r == t)
        def _():
            pltpu.make_async_copy(out_buf.at[t], out.at[:, columns], own_sem.at[1]).start()

    tri = lax.broadcasted_iota(jnp.int32, (tok, tok), 0) >= lax.broadcasted_iota(
        jnp.int32, (tok, tok), 1
    )

    def attend(t):
        own = slice(t * tok, (t + 1) * tok)
        first = (t + 1) * tok
        bias_own = hidden_bias(0, t * tok, (begins[t] - base) * tok) if t else None
        bias_prev = (
            hidden_bias(first, (GROUP - 1 - t) * tok, (begins[t] - base + GROUP) * tok)
            if t < GROUP - 1
            else None
        )

        def one_head(hh, carry):
            q = q_own[hh, own, :]
            parts = [(jnp.where(tri, score(q, k_own[hh, own, :]), NEG), v_own[hh, own, :])]
            if t:
                parts.append((score(q, k_own[hh, : t * tok, :]) + bias_own, v_own[hh, : t * tok, :]))
            if t < GROUP - 1:
                parts.append((score(q, k_prev[hh, first:, :]) + bias_prev, v_prev[hh, first:, :]))
            top = functools.reduce(
                jnp.maximum, [jnp.max(part, axis=-1, keepdims=True) for part, _ in parts]
            )
            total = 0.0
            acc = 0.0
            for part, values in parts:
                exps = jnp.exp2((part - top) * slope)
                total = total + jnp.sum(exps, axis=-1, keepdims=True)
                acc = acc + jnp.dot(exps.astype(BF16), values, preferred_element_type=F32)
            finish(hh, t, acc, total)
            return carry

        lax.fori_loop(0, per, one_head, 0, unroll=True)

    attend(GROUP - 1)
    send_out(GROUP - 1)

    def take_prev(j):
        remote(res_own.at[j], res_prev.at[j], next_send.at[j], prev_recv.at[j], me).wait_recv()

    def project_prev(j):
        scales = jnp.transpose(jnp.broadcast_to(sc_prev[j][0:1], (tok, tok)))
        tile = res_prev[j]
        rows = slice(j * tok, (j + 1) * tok)
        for hh in range(per):
            normed = norm_head(tile, scales, hh)
            made = jnp.dot(normed, w_attn[hh][:, hd:], preferred_element_type=F32).astype(BF16)
            k_prev[hh, rows, :] = made[:, :hd]
            v_prev[hh, rows, :] = made[:, hd:]

    @pl.when(has_prev)
    def _():
        scales_on.wait_recv()
        for j in range(1, GROUP):
            take_prev(j)
        for j in range(1, GROUP):
            project_prev(j)

    @pl.when(jnp.logical_not(has_prev))
    def _():
        k_prev[...] = jnp.zeros_like(k_prev)
        v_prev[...] = jnp.zeros_like(v_prev)

    def attend_step(step, carry):
        tile = lax.rem(r + 1 + step, GROUP)
        for t in range(GROUP - 1):
            pl.when(tile == t)(functools.partial(attend, t))

        @pl.when(tile < GROUP - 1)
        def _():
            send_out(tile)

        return carry

    lax.fori_loop(0, GROUP, attend_step, 0)

    @pl.when(me < ctx - 1)
    def _():
        halo.wait_send()

    @pl.when(has_next)
    def _():
        scales_on.wait_send()

    def drain(j, carry):
        @pl.when(has_next & (j > 0))
        def _():
            remote(res_own.at[j], res_prev.at[j], next_send.at[j], prev_recv.at[j], me).wait_send()

        @pl.when(j != r)
        def _():
            remote(res_send.at[j], res_own.at[r], own_send.at[j], own_recv.at[r], base + j).wait_send()
            remote(sc_send, sc_own.at[r], own_sc_send.at[j], own_sc_recv.at[r], base + j).wait_send()
            columns = pl.ds(pl.multiple_of(j * wide, wide), wide)
            sent = remote(out_buf.at[j], out.at[:, columns], out_send.at[j], out_recv.at[j], base + j)
            sent.wait_send()
            sent.wait_recv()

        @pl.when(j == r)
        def _():
            columns = pl.ds(pl.multiple_of(r * wide, wide), wide)
            pltpu.make_async_copy(out_buf.at[j], out.at[:, columns], own_sem.at[1]).wait()

        return carry

    lax.fori_loop(0, GROUP, drain, 0)


def shards(ctx, hidden_in, in_weight, feat_filter, inner_filter, norm_gain, attn_weight, doc_lengths):
    tok, channels = hidden_in.shape
    heads, hd, _ = in_weight.shape
    per = heads // GROUP
    wide = per * hd
    span = GROUP * tok
    any_spec = pl.BlockSpec(memory_space=pl.ANY)
    dma = pltpu.SemaphoreType.DMA
    return pl.pallas_call(
        functools.partial(kernel, ctx),
        out_shape=jax.ShapeDtypeStruct((tok, channels), BF16),
        in_specs=[
            pl.BlockSpec(memory_space=pltpu.SMEM),
            any_spec,
            any_spec,
            any_spec,
            any_spec,
            any_spec,
            any_spec,
        ],
        out_specs=any_spec,
        scratch_shapes=[
            pltpu.VMEM((HALO + tok, channels), BF16),
            pltpu.VMEM(feat_filter.shape, F32),
            pltpu.VMEM(inner_filter.shape, F32),
            pltpu.VMEM((1, channels), F32),
            pltpu.VMEM((heads, hd, 3 * hd), BF16),
            pltpu.VMEM((per, hd, 3 * hd), BF16),
            pltpu.VMEM((GROUP, tok, wide), BF16),
            pltpu.VMEM((GROUP, tok, wide), BF16),
            pltpu.VMEM((GROUP, tok, wide), BF16),
            pltpu.VMEM((8, tok), F32),
            pltpu.VMEM((GROUP, 8, tok), F32),
            pltpu.VMEM((GROUP, 8, tok), F32),
            pltpu.VMEM((tok, hd), F32),
            pltpu.VMEM((per, span, hd), BF16),
            pltpu.VMEM((per, span, hd), BF16),
            pltpu.VMEM((per, span, hd), BF16),
            pltpu.VMEM((per, span, hd), BF16),
            pltpu.VMEM((per, span, hd), BF16),
            pltpu.VMEM((GROUP, tok, wide), BF16),
            dma((8,)),
            dma((2,)),
        ]
        + [dma((GROUP,))] * 10
        + [dma((2,))],
        compiler_params=pltpu.CompilerParams(
            collective_id=0, has_side_effects=True, vmem_limit_bytes=56 * 1024 * 1024
        ),
        cost_estimate=pl.CostEstimate(
            flops=6_000_000_000, bytes_accessed=9_000_000, transcendentals=4_200_000
        ),
    )(
        doc_lengths,
        hidden_in,
        in_weight,
        feat_filter,
        inner_filter,
        norm_gain.reshape(1, channels),
        attn_weight,
    )


def solution(mesh):
    return jax.shard_map(
        functools.partial(shards, mesh.shape["ctx"]),
        mesh=mesh,
        in_specs=(P(("groups", "ctx"), None), P(), P(), P(), P(), P(), P("groups")),
        out_specs=P(("groups", "ctx"), None),
        check_vma=False,
    )
```
